128 devices in a mesh: seq: 32 (over z, x, y_hi), head: 4 (over y_lo, core).
Axes of the slice: x: 4, y: 4 (y_hi: 2, y_lo: 2; y = y_hi * 2 + y_lo), z: 4, core: 2. Of those that a mesh axis runs over, the one named last changes fastest.
Arguments:
- video_query: bfloat16 [16384, 3072], P(('seq', 'head')), may hold values from -16 to 16
- audio_key: bfloat16 [16384, 3072], P(('seq', 'head')), may hold values from -16 to 16
- audio_value: bfloat16 [16384, 3072], P(('seq', 'head')), may hold values from -6 to 6
- grad_out: bfloat16 [16384, 3072], P(('seq', 'head')), may hold values from -6 to 6
- audio_time: int32 [16384], P(('seq', 'head')), may hold values from -1 to 19999, as said below
Outputs:
- attended: bfloat16 [16384, 3072], P(('seq', 'head'))
- grad_query: bfloat16 [16384, 3072], P(('seq', 'head'))
- grad_key: bfloat16 [16384, 3072], P(('seq', 'head'))
- grad_value: bfloat16 [16384, 3072], P(('seq', 'head'))
The draws below stay inside these ranges and needn't reach their ends.
Inputs may be any that keep to these rules, and one draw needn't show every extreme that they name: `audio_time`: slots r * 512 to (r+1) * 512 - 1 belong to time range r: their live slots come first, with stamps from r * 625 to (r+1) * 625 - 1 in rising order, and the rest hold -1. Every range has at least 170 live slots, and in every draw some range has all 512 live.
All inputs are finite; a program needn't handle non-finite values.
Results may differ from the reference program's by a relative error of at most 0.0061.
Values may be sent and summed in bfloat16 or wider, within the bound.
No kernel may reach another device: no remote copies, remote signals or barrier semaphores. Data moves between devices by JAX's collectives and lax.ppermute only.
A program may use at most 192 MiB of HBM per device.

```python
import jax
import jax.numpy as jnp
from jax import lax

D = 3072
HEADS = 24
DH = 128
SHARD_MS = 625
RADIUS_MS = 1000
VSEQ = 512
CAP = 512
NV = 16384
NA = 16384
N_SEQ = 32


def draw_video_query(key, part):
    base = jax.random.normal(jax.random.fold_in(key, 11), (NV, D), jnp.float32)
    base = jnp.clip(base, -6.0, 6.0)
    return base.astype(jnp.bfloat16)


def draw_audio_key(key, part):
    base = jax.random.normal(jax.random.fold_in(key, 21), (NA, D), jnp.float32)
    base = jnp.clip(base, -6.0, 6.0)
    return base.astype(jnp.bfloat16)


def draw_audio_time(key, part):
    range_count = NA // CAP
    counts = jax.random.randint(jax.random.fold_in(key, 31), (range_count,), CAP // 3, CAP + 1)
    busiest = jax.random.randint(jax.random.fold_in(key, 32), (), 0, range_count)
    counts = counts.at[busiest].set(CAP)
    offsets = jax.random.randint(jax.random.fold_in(key, 33), (range_count, CAP), 0, SHARD_MS)
    slot_ids = jnp.arange(CAP, dtype=jnp.int32)[None, :]
    live = slot_ids < counts[:, None]
    ordered = jnp.sort(jnp.where(live, offsets, SHARD_MS + 1), axis=1)
    starts = (jnp.arange(range_count, dtype=jnp.int32) * SHARD_MS)[:, None]
    stamps = jnp.where(live, starts + ordered, -1)
    return stamps.reshape(NA).astype(jnp.int32)


def block_scale(key, shape, split, least, top_value):
    factor_of, own = 1.0, jax.random.fold_in(key, 6)
    for position, parts in split:
        draws = jnp.exp(jax.random.uniform(jax.random.fold_in(own, position), (parts,), jnp.float32, least / len(split), top_value / len(split)))
        factor_of = factor_of * jnp.repeat(draws, shape[position] // parts).reshape([-1 if axis == position else 1 for axis in range(len(shape))])
    return factor_of


def noise(rng, dims, scale, limit, shards=(), kind=jnp.bfloat16):
    loudness = block_scale(rng, dims, shards, -0.22, 0.18) if shards else 1.0
    values = jax.random.normal(rng, dims, jnp.float32) * scale * loudness
    return jnp.minimum(jnp.maximum(values, -limit), limit).astype(kind)


def setup_inputs(seed: int = 0) -> dict:
    splits = jax.random.split(jax.random.key(seed), 6)
    return {
        "video_query": draw_video_query(jax.random.fold_in(splits[5], 71), 0),
        "audio_key": draw_audio_key(jax.random.fold_in(splits[5], 71), 0),
        "audio_value": noise(splits[2], (NA, D), 1.0, 6.0, ((0, 128),)),
        "grad_out": noise(splits[3], (NV, D), 1.0, 6.0, ((0, 128),)),
        "audio_time": draw_audio_time(jax.random.fold_in(splits[5], 71), 0),
    }


NEG_FILL = -1e30


def attend_block(query_rows, key_rows, value_rows, grad_rows, query_stamps, key_stamps):
    scaling = DH ** -0.5
    allowed = (key_stamps[None, :] >= 0) & (jnp.abs(query_stamps[:, None] - key_stamps[None, :]) <= RADIUS_MS)
    query_float = query_rows.astype(jnp.float32)
    key_float = key_rows.astype(jnp.float32)
    value_float = value_rows.astype(jnp.float32)
    grad_float = grad_rows.astype(jnp.float32)
    scores = jnp.einsum("qhd,khd->hqk", query_float, key_float) * scaling
    scores = jnp.where(allowed[None], scores, NEG_FILL)
    row_max = jnp.max(scores, axis=2, keepdims=True)
    row_total = jnp.sum(jnp.exp(scores - row_max), axis=2, keepdims=True)
    log_total = row_max + jnp.log(row_total)
    weights = jnp.exp(scores - log_total)
    weights_low = weights.astype(jnp.bfloat16).astype(jnp.float32)
    attended_full = jnp.einsum("hqk,khd->qhd", weights_low, value_float)
    row_dot = jnp.sum(grad_float * attended_full, axis=2)
    grad_weights = jnp.einsum("qhd,khd->hqk", grad_float, value_float)
    grad_scores = (weights * (grad_weights - row_dot.T[:, :, None])).astype(jnp.bfloat16).astype(jnp.float32)
    grad_query = jnp.einsum("hqk,khd->qhd", grad_scores, key_float) * scaling
    grad_key = jnp.einsum("hqk,qhd->khd", grad_scores, query_float) * scaling
    grad_value = jnp.einsum("hqk,qhd->khd", weights_low, grad_float)
    return attended_full, grad_query, grad_key, grad_value


def reference(video_query, audio_key, audio_value, grad_out, audio_time):
    model_width = video_query.shape[1]
    pad_rows = 2 * CAP
    zero_rows = jnp.zeros((pad_rows, model_width), audio_key.dtype)
    key_padded = jnp.concatenate([zero_rows, audio_key, zero_rows], 0)
    value_padded = jnp.concatenate([zero_rows, audio_value, zero_rows], 0)
    stamp_fill = jnp.full((pad_rows,), -1, jnp.int32)
    stamp_padded = jnp.concatenate([stamp_fill, audio_time.astype(jnp.int32), stamp_fill], 0)
    offsets = (jnp.arange(VSEQ, dtype=jnp.int32) * SHARD_MS) // VSEQ

    def per_range(running, range_index):
        key_sums, value_sums = running
        row_start = (range_index * VSEQ).astype(jnp.int32)
        slot_start = (range_index * CAP).astype(jnp.int32)
        query_rows = lax.dynamic_slice_in_dim(video_query, row_start, VSEQ, 0).reshape(VSEQ, HEADS, DH)
        grad_rows = lax.dynamic_slice_in_dim(grad_out, row_start, VSEQ, 0).reshape(VSEQ, HEADS, DH)
        key_rows = lax.dynamic_slice_in_dim(key_padded, slot_start, 5 * CAP, 0).reshape(5 * CAP, HEADS, DH)
        value_rows = lax.dynamic_slice_in_dim(value_padded, slot_start, 5 * CAP, 0).reshape(5 * CAP, HEADS, DH)
        key_stamps = lax.dynamic_slice_in_dim(stamp_padded, slot_start, 5 * CAP, 0)
        query_stamps = (range_index * SHARD_MS).astype(jnp.int32) + offsets
        attended_full, grad_query, grad_key, grad_value = attend_block(
            query_rows, key_rows, value_rows, grad_rows, query_stamps, key_stamps)
        old_keys = lax.dynamic_slice_in_dim(key_sums, slot_start, 5 * CAP, 0)
        key_sums = lax.dynamic_update_slice_in_dim(key_sums, old_keys + grad_key.reshape(5 * CAP, model_width), slot_start, 0)
        old_values = lax.dynamic_slice_in_dim(value_sums, slot_start, 5 * CAP, 0)
        value_sums = lax.dynamic_update_slice_in_dim(value_sums, old_values + grad_value.reshape(5 * CAP, model_width), slot_start, 0)
        outputs = (attended_full.reshape(VSEQ, model_width).astype(jnp.bfloat16),
                   grad_query.reshape(VSEQ, model_width).astype(jnp.bfloat16))
        return (key_sums, value_sums), outputs

    zero_sums = (jnp.zeros((NA + 4 * CAP, model_width), jnp.float32),
                 jnp.zeros((NA + 4 * CAP, model_width), jnp.float32))
    (key_sums, value_sums), (attended, grad_query) = lax.scan(
        per_range, zero_sums, jnp.arange(N_SEQ, dtype=jnp.int32))
    grad_key = key_sums[pad_rows:pad_rows + NA].astype(jnp.bfloat16)
    grad_value = value_sums[pad_rows:pad_rows + NA].astype(jnp.bfloat16)
    return (attended.reshape(NV, model_width), grad_query.reshape(NV, model_width), grad_key, grad_value)
```

```python
import functools
import math

import jax
import jax.numpy as jnp
from jax import lax
from jax.experimental import pallas as pl
from jax.experimental.pallas import tpu as pltpu
from jax.sharding import Mesh
from jax.sharding import PartitionSpec as P

DH = 128
SHARD_MS = 625
RADIUS_MS = 1000
NEG_FILL = -1e30
FAR = -1e6
SCALE = DH ** (-0.5)
LOG2E = 1.4426950408889634
GROUP = ("yh", "head")
CHUNKS = ((0,), (1,), (2,))
RANGES = 2
REACH = 2
VMEM_BYTES = 56 * 1024 * 1024


def dot(lhs, rhs, dims):
    return lax.dot_general(lhs, rhs, (dims, ((), ())), preferred_element_type=jnp.float32)


def dot_nn(lhs, rhs):
    return dot(lhs, rhs, ((1,), (0,)))


def dot_nt(lhs, rhs):
    return dot(lhs, rhs, ((1,), (1,)))


def pack_kernel(peers, heads, chunks, a_ref, b_ref, *outs):
    for out, chunk in zip(outs, chunks):
        for peer in range(peers):
            for place, head in enumerate(chunk):
                lanes = pl.ds((peer * heads + head) * DH, DH)
                out[peer, place, 0] = a_ref[:, lanes]
                out[peer, place, 1] = b_ref[:, lanes]


def pack(first, second, peers, chunks):
    rows, width = first.shape
    heads = width // DH // peers
    return pl.pallas_call(
        functools.partial(pack_kernel, peers, heads, chunks),
        out_shape=[
            jax.ShapeDtypeStruct((peers, len(chunk), 2, rows, DH), first.dtype) for chunk in chunks
        ],
        compiler_params=pltpu.CompilerParams(vmem_limit_bytes=VMEM_BYTES),
        name="pack",
    )(first, second)


def unpack_kernel(peers, heads, chunks, *refs):
    ins, (a_ref, b_ref) = refs[: len(chunks)], refs[len(chunks) :]
    for piece, chunk in zip(ins, chunks):
        for peer in range(peers):
            for place, head in enumerate(chunk):
                lanes = pl.ds((peer * heads + head) * DH, DH)
                a_ref[:, lanes] = piece[peer, place, 0]
                b_ref[:, lanes] = piece[peer, place, 1]


def unpack(pieces, chunks):
    peers, _, _, rows, _ = pieces[0].shape
    heads = sum(len(chunk) for chunk in chunks)
    shape = jax.ShapeDtypeStruct((rows, peers * heads * DH), pieces[0].dtype)
    return pl.pallas_call(
        functools.partial(unpack_kernel, peers, heads, chunks),
        out_shape=[shape, shape],
        compiler_params=pltpu.CompilerParams(vmem_limit_bytes=VMEM_BYTES),
        name="unpack",
    )(*pieces)


def attend_kernel(
    per, size, stamps_ref, qg_ref, left_ref, own_ref, right_ref,
    result_ref, to_left_ref, own_sum_ref, to_right_ref,
    keys, values, keys_t, values_t, scores, grad_weights, key_sums, value_sums, total_t, query_t,
):
    span = 2 * REACH + 1
    for side, ref in enumerate((left_ref, own_ref, right_ref)):
        for part in range(RANGES):
            place = side * RANGES + part
            rows = pl.ds(part * per, per)
            key_tile = ref[rows, 0, 0].reshape(size, DH)
            value_tile = ref[rows, 0, 1].reshape(size, DH)
            keys[place] = key_tile
            values[place] = value_tile
            keys_t[place] = key_tile.T
            values_t[place] = value_tile.T
    key_sums[...] = jnp.zeros_like(key_sums)
    value_sums[...] = jnp.zeros_like(value_sums)
    offsets = lax.broadcasted_iota(jnp.int32, (1, size), 1) * SHARD_MS // size
    for part in range(RANGES):
        rows = pl.ds(part * per, per)
        query = qg_ref[rows, 0, 0].reshape(size, DH)
        grad = qg_ref[rows, 0, 1].reshape(size, DH)
        stamp = (offsets + part * SHARD_MS).astype(jnp.float32)

        def score_step(step, top):
            place = step + part
            found = dot_nt(keys[place], query)
            near = jnp.abs(jnp.tile(stamps_ref[place], (1, size // DH)) - stamp) <= RADIUS_MS
            found = jnp.where(near, found * (SCALE * LOG2E), NEG_FILL)
            scores[step] = found
            return jnp.maximum(top, jnp.max(found.reshape(size // 8, 8, size), axis=0))

        top = lax.fori_loop(0, span, score_step, jnp.full((8, size), NEG_FILL, jnp.float32))
        top = jnp.max(top, axis=0, keepdims=True)
        total_t[...] = jnp.zeros_like(total_t)

        def weight_step(step, total):
            place = step + part
            raised = jnp.exp2(scores[step] - top)
            scores[step] = raised
            total_t[...] += dot_nn(values_t[place], raised.astype(jnp.bfloat16))
            grad_weights[step] = dot_nt(values[place], grad)
            return total + jnp.sum(raised.reshape(size // 8, 8, size), axis=0)

        total = lax.fori_loop(0, span, weight_step, jnp.zeros((8, size), jnp.float32))
        inverse = 1.0 / jnp.sum(total, axis=0, keepdims=True)
        attended_t = total_t[...] * inverse
        row_dot = jnp.sum(attended_t * grad.astype(jnp.float32).T, axis=0, keepdims=True)
        result_ref[rows, 0, 0] = attended_t.T.astype(jnp.bfloat16).reshape(per, size // per, DH)
        query_t[...] = jnp.zeros_like(query_t)

        def grad_step(step, carry):
            place = step + part
            weights = scores[step] * inverse
            slopes = (weights * (grad_weights[step] - row_dot)).astype(jnp.bfloat16)
            value_sums[place] += dot_nn(weights.astype(jnp.bfloat16), grad)
            key_sums[place] += dot_nn(slopes, query)
            query_t[...] += dot_nn(keys_t[place], slopes)
            return carry

        lax.fori_loop(0, span, grad_step, 0)
        result_ref[rows, 0, 1] = (
            (query_t[...] * SCALE).T.astype(jnp.bfloat16).reshape(per, size // per, DH)
        )
    for side, ref in enumerate((to_left_ref, own_sum_ref, to_right_ref)):
        for part in range(RANGES):
            place = side * RANGES + part
            rows = pl.ds(part * per, per)
            shape = (per, size // per, DH)
            ref[rows, 0, 0] = (key_sums[place] * SCALE).astype(ref.dtype).reshape(shape)
            ref[rows, 0, 1] = value_sums[place].astype(ref.dtype).reshape(shape)


def attend(stamps, query_grad, left, own, right):
    peers, heads, _, rows, _ = own.shape
    per = peers // RANGES
    size = per * rows
    span = 2 * REACH + 1
    places = 3 * RANGES
    piece = pl.BlockSpec((peers, 1, 2, rows, DH), lambda head: (0, head, 0, 0, 0))
    low = jax.ShapeDtypeStruct(own.shape, jnp.bfloat16)
    wide = jax.ShapeDtypeStruct(own.shape, jnp.float32)
    pairs = RANGES * span * size * size * heads
    return pl.pallas_call(
        functools.partial(attend_kernel, per, size),
        grid=(heads,),
        in_specs=[pl.BlockSpec((places, size, DH), lambda head: (0, 0, 0))] + [piece] * 4,
        out_specs=[piece] * 4,
        out_shape=[low, low, wide, low],
        scratch_shapes=[
            pltpu.VMEM((places, size, DH), jnp.bfloat16),
            pltpu.VMEM((places, size, DH), jnp.bfloat16),
            pltpu.VMEM((places, DH, size), jnp.bfloat16),
            pltpu.VMEM((places, DH, size), jnp.bfloat16),
            pltpu.VMEM((span, size, size), jnp.float32),
            pltpu.VMEM((span, size, size), jnp.float32),
            pltpu.VMEM((places, size, DH), jnp.float32),
            pltpu.VMEM((places, size, DH), jnp.float32),
            pltpu.VMEM((DH, size), jnp.float32),
            pltpu.VMEM((DH, size), jnp.float32),
        ],
        compiler_params=pltpu.CompilerParams(vmem_limit_bytes=VMEM_BYTES),
        cost_estimate=pl.CostEstimate(
            flops=pairs * DH * 12, bytes_accessed=16 * own.size, transcendentals=pairs
        ),
        name="attend",
    )(stamps, query_grad, left, own, right)


def swap(value):
    return lax.all_to_all(value, GROUP, split_axis=0, concat_axis=0, tiled=True)


def shifted(value, steps):
    count = lax.axis_size("col")
    first, last = max(0, -steps), min(count, count - steps)
    return lax.ppermute(value, "col", [(at, at + steps) for at in range(first, last)])


def on_device(video_query, audio_key, audio_value, grad_out, audio_time):
    peers = lax.axis_size(GROUP)
    key_values = pack(audio_key, audio_value, peers, CHUNKS)
    query_grads = pack(video_query, grad_out, peers, CHUNKS)
    lifted = lax.all_gather(audio_time, GROUP, axis=0, tiled=True) + 1
    window = jnp.concatenate([shifted(lifted, 1), lifted, shifted(lifted, -1)]) - 1
    base = lax.axis_index("col") * (RANGES * SHARD_MS)
    stamps = jnp.where(window >= 0, (window - base).astype(jnp.float32), FAR)
    size = lifted.shape[0] // RANGES
    stamps = jnp.broadcast_to(stamps[:, None], (stamps.shape[0], DH)).reshape(-1, size, DH)
    results, grads = [], []
    for key_value, query_grad in zip(key_values, query_grads):
        own = swap(key_value)
        left, right = shifted(own, 1), shifted(own, -1)
        result, to_left, own_sum, to_right = attend(stamps, swap(query_grad), left, own, right)
        results.append(swap(result))
        summed = (
            own_sum
            + shifted(to_left, -1).astype(jnp.float32)
            + shifted(to_right, 1).astype(jnp.float32)
        )
        grads.append(swap(summed.astype(jnp.bfloat16)))
    attended, grad_query = unpack(results, CHUNKS)
    grad_key, grad_value = unpack(grads, CHUNKS)
    return attended, grad_query, grad_key, grad_value


def solution(mesh):
    columns = mesh.shape["seq"] // RANGES
    split = Mesh(
        mesh.devices.reshape(columns, RANGES, mesh.shape["head"]), ("col", "yh", "head")
    )
    rows = P(("col", "yh", "head"), None)
    return jax.shard_map(
        on_device,
        mesh=split,
        in_specs=(rows, rows, rows, rows, P(("col", "yh", "head"))),
        out_specs=(rows, rows, rows, rows),
        check_vma=False,
    )
```

```python
import functools
import math

import jax
import jax.numpy as jnp
from jax import lax
from jax.experimental import pallas as pl
from jax.experimental.pallas import tpu as pltpu
from jax.sharding import Mesh
from jax.sharding import PartitionSpec as P

DH = 128
SHARD_MS = 625
RADIUS_MS = 1000
NEG_FILL = -1e30
FAR = -1e6
SCALE = DH ** (-0.5)
LOG2E = 1.4426950408889634
GROUP = ("yh", "head")
CHUNKS = ((0, 1), (2,))
STAMP_ROWS = 16
STAMP_BASE = 32
RANGES = 2
UNROLL = True
REACH = 2
VMEM_BYTES = 56 * 1024 * 1024


def dot(lhs, rhs, dims):
    return lax.dot_general(lhs, rhs, (dims, ((), ())), preferred_element_type=jnp.float32)


def dot_nn(lhs, rhs):
    return dot(lhs, rhs, ((1,), (0,)))


def dot_nt(lhs, rhs):
    return dot(lhs, rhs, ((1,), (1,)))


def pack_kernel(peers, heads, plans, stamped, count, *refs):
    ins, outs = refs[:count], refs[count + stamped :]
    rows = ins[0].shape[0]
    for number, (out, plan) in enumerate(zip(outs, plans)):
        for peer in range(peers):
            for at, (which, head) in enumerate(plan):
                lanes = pl.ds((peer * heads + head) * DH, DH)
                out[peer, pl.ds(at * rows, rows)] = ins[which][:, lanes]
            if stamped and number == 0:
                out[peer, pl.ds(len(plan) * rows, STAMP_ROWS)] = refs[count][...]


def pack(arrays, plans, peers, stamp_rows=None):
    rows, width = arrays[0].shape
    stamps = [] if stamp_rows is None else [stamp_rows]
    extra = [STAMP_ROWS if stamps and number == 0 else 0 for number in range(len(plans))]
    return pl.pallas_call(
        functools.partial(
            pack_kernel, peers, width // DH // peers, plans, len(stamps), len(arrays)
        ),
        out_shape=[
            jax.ShapeDtypeStruct((peers, len(plan) * rows + more, DH), arrays[0].dtype)
            for plan, more in zip(plans, extra)
        ],
        compiler_params=pltpu.CompilerParams(vmem_limit_bytes=VMEM_BYTES),
        name="pack",
    )(*arrays, *stamps)


def place_kernel(peers, heads, chunk, offsets, *refs):
    count = len(offsets)
    pieces, outs, sems = refs[:count], refs[-2 * count - 1 : -1], refs[-1]
    rows = outs[0].shape[0]
    copies = []
    for piece, offset, pair in zip(pieces, offsets, zip(outs[::2], outs[1::2])):
        for peer in range(peers):
            for place, head in enumerate(chunk):
                lanes = pl.ds((peer * heads + head) * DH, DH)
                for which, out in enumerate(pair):
                    start = offset + (2 * place + which) * rows
                    copies.append(
                        pltpu.make_async_copy(
                            piece.at[peer, pl.ds(start, rows)],
                            out.at[:, lanes],
                            sems.at[len(copies)],
                        )
                    )
    for copy in copies:
        copy.start()
    for copy in copies:
        copy.wait()


def place(pieces, offsets, chunk, heads, rows, outs):
    peers = pieces[0].shape[0]
    shape = jax.ShapeDtypeStruct((rows, peers * heads * DH), pieces[0].dtype)
    number = 2 * len(pieces)
    anywhere = pl.BlockSpec(memory_space=pl.ANY)
    return pl.pallas_call(
        functools.partial(place_kernel, peers, heads, chunk, offsets),
        in_specs=[pl.BlockSpec(memory_space=pltpu.VMEM)] * len(pieces) + [anywhere] * len(outs),
        out_specs=[anywhere] * number,
        out_shape=[shape] * number,
        input_output_aliases={len(pieces) + at: at for at in range(len(outs))},
        scratch_shapes=[pltpu.SemaphoreType.DMA((number * peers * len(chunk),))],
        compiler_params=pltpu.CompilerParams(vmem_limit_bytes=VMEM_BYTES),
        name="place",
    )(*pieces, *outs)


def spread_stamps(codes, shift):
    size = codes.shape[1]
    place = lax.broadcasted_iota(jnp.int32, (size, size), 0)
    diagonal = place == lax.broadcasted_iota(jnp.int32, (size, size), 1)
    ones = jnp.ones((size, size), jnp.bfloat16)
    found = [
        dot_nn(jnp.where(diagonal, codes[row : row + 1].astype(jnp.float32), 0.0).astype(jnp.bfloat16), ones)
        for row in range(2)
    ]
    code = found[0] * STAMP_BASE + found[1]
    return jnp.where(code > 0.5, code + (shift - 1), FAR)


def attend_kernel(
    per, size, fresh,
    stamps_left, stamps_own, stamps_right, qg_ref, left_ref, own_ref, right_ref, *refs
):
    skip = 4 - sum(fresh)
    result_ref, to_left_ref, own_sum_ref, to_right_ref = refs[skip : skip + 4]
    (
        stamps, keys, values, keys_t, values_t,
        scores, grad_weights, key_sums, value_sums, total_t, query_t,
    ) = refs[skip + 4 :]
    rows = size // per
    span = 2 * REACH + 1

    @pl.when(pl.program_id(0) == 0)
    def _():
        for side, ref in enumerate((stamps_left, stamps_own, stamps_right)):
            for block in range(RANGES * per):
                place = side * RANGES + block // per
                spread = spread_stamps(ref[block], (place - RANGES) * SHARD_MS)
                stamps[place, pl.ds(block % per * rows, rows)] = spread

    for side, ref in enumerate((left_ref, own_ref, right_ref)):
        for part in range(RANGES):
            place = side * RANGES + part
            blocks = pl.ds(part * per, per)
            key_tile = ref[blocks, pl.ds(0, rows)].reshape(size, DH)
            value_tile = ref[blocks, pl.ds(rows, rows)].reshape(size, DH)
            keys[place] = key_tile
            values[place] = value_tile
            keys_t[place] = key_tile.T
            values_t[place] = value_tile.T
    key_sums[...] = jnp.zeros_like(key_sums)
    value_sums[...] = jnp.zeros_like(value_sums)
    total_t[...] = jnp.zeros_like(total_t)
    query_t[...] = jnp.zeros_like(query_t)
    offsets = lax.broadcasted_iota(jnp.int32, (1, size), 1) * SHARD_MS // size
    blocks = [pl.ds(part * per, per) for part in range(RANGES)]
    query = [qg_ref[block, pl.ds(0, rows)].reshape(size, DH) for block in blocks]
    grad = [qg_ref[block, pl.ds(rows, rows)].reshape(size, DH) for block in blocks]
    stamp = [(offsets + part * SHARD_MS).astype(jnp.float32) for part in range(RANGES)]
    top, inverse, row_dot = [None] * RANGES, [None] * RANGES, [None] * RANGES

    def score_step(part, step, top):
        place = step + part
        found = dot_nt(keys[place], query[part])
        near = jnp.abs(jnp.tile(stamps[place], (1, size // DH)) - stamp[part]) <= RADIUS_MS
        found = jnp.where(near, found * (SCALE * LOG2E), NEG_FILL)
        scores[part, step] = found
        return jnp.maximum(top, jnp.max(found.reshape(size // 8, 8, size), axis=0))

    def weight_step(part, step, total):
        place = step + part
        raised = jnp.exp2(scores[part, step] - top[part])
        scores[part, step] = raised
        total_t[part] += dot_nn(values_t[place], raised.astype(jnp.bfloat16))
        return total + jnp.sum(raised.reshape(size // 8, 8, size), axis=0)

    def grad_step(part, step):
        place = step + part
        weights = scores[part, step] * inverse[part]
        slopes = (weights * (dot_nt(values[place], grad[part]) - row_dot[part])).astype(jnp.bfloat16)
        value_sums[place] += dot_nn(weights.astype(jnp.bfloat16), grad[part])
        key_sums[place] += dot_nn(slopes, query[part])
        query_t[part] += dot_nn(keys_t[place], slopes)

    def finish(part, total):
        inverse[part] = 1.0 / jnp.sum(total, axis=0, keepdims=True)
        attended_t = total_t[part] * inverse[part]
        row_dot[part] = jnp.sum(
            attended_t * grad[part].astype(jnp.float32).T, axis=0, keepdims=True
        )
        shape = (per, rows, DH)
        result_ref[blocks[part], pl.ds(0, rows)] = attended_t.T.astype(jnp.bfloat16).reshape(shape)

    def finish_query(part):
        low = (query_t[part] * SCALE).T.astype(jnp.bfloat16)
        result_ref[blocks[part], pl.ds(rows, rows)] = low.reshape(per, rows, DH)

    lowest = jnp.full((8, size), NEG_FILL, jnp.float32)
    zero = jnp.zeros((8, size), jnp.float32)
    found = lax.fori_loop(0, span, lambda step, c: score_step(0, step, c), lowest, unroll=UNROLL)
    top[0] = jnp.max(found, axis=0, keepdims=True)

    def second(step, carry):
        return weight_step(0, step, carry[0]), score_step(1, step, carry[1])

    total, found = lax.fori_loop(0, span, second, (zero, lowest), unroll=UNROLL)
    top[1] = jnp.max(found, axis=0, keepdims=True)
    finish(0, total)

    def third(step, carry):
        grad_step(0, step)
        return weight_step(1, step, carry)

    total = lax.fori_loop(0, span, third, zero, unroll=UNROLL)
    finish_query(0)
    finish(1, total)

    def fourth(step, carry):
        grad_step(1, step)
        return carry

    lax.fori_loop(0, span, fourth, 0, unroll=UNROLL)
    finish_query(1)
    for side, ref in enumerate((to_left_ref, own_sum_ref, to_right_ref)):
        for part in range(RANGES):
            place = side * RANGES + part
            shape = (per, rows, DH)
            ref[blocks[part], pl.ds(0, rows)] = (key_sums[place] * SCALE).astype(ref.dtype).reshape(shape)
            ref[blocks[part], pl.ds(rows, rows)] = value_sums[place].astype(ref.dtype).reshape(shape)


def attend(heads, stamped, query_grad, sides, result, sums, sizes):
    peers = stamped[0].shape[0]
    per = peers // RANGES
    rows = (stamped[0].shape[1] - STAMP_ROWS) // (2 * len(CHUNKS[0]))
    size = per * rows
    span = 2 * REACH + 1
    places = 3 * RANGES

    def piece(first):
        start = heads[0] - first
        return pl.BlockSpec((peers, 2 * rows, DH), lambda head: (0, start + head, 0))

    stamp_block = 2 * len(CHUNKS[0]) * rows // STAMP_ROWS
    stamp_spec = pl.BlockSpec((peers, STAMP_ROWS, DH), lambda head: (0, stamp_block, 0))
    old = [result[0], *sums[0]]
    firsts = [result[1]] + [sums[1]] * 3
    kinds = [jnp.bfloat16] * 4
    counts = [sizes[0]] + [sizes[1]] * 3
    fresh = [value is None for value in old]
    operands = [*stamped, query_grad[0], *sides[0]]
    in_specs = [stamp_spec] * 3 + [piece(first) for first in (query_grad[1], *sides[1])]
    aliases = {}
    for number, value in enumerate(old):
        if value is not None:
            aliases[len(operands)] = number
            operands.append(value)
            in_specs.append(pl.BlockSpec(memory_space=pl.ANY))

    return pl.pallas_call(
        functools.partial(attend_kernel, per, size, fresh),
        grid=(len(heads),),
        in_specs=in_specs,
        out_specs=[piece(first) for first in firsts],
        out_shape=[
            jax.ShapeDtypeStruct((peers, 2 * rows * count, DH), kind)
            for count, kind in zip(counts, kinds)
        ],
        input_output_aliases=aliases,
        scratch_shapes=[
            pltpu.VMEM((places, size, DH), jnp.float32),
            pltpu.VMEM((places, size, DH), jnp.bfloat16),
            pltpu.VMEM((places, size, DH), jnp.bfloat16),
            pltpu.VMEM((places, DH, size), jnp.bfloat16),
            pltpu.VMEM((places, DH, size), jnp.bfloat16),
            pltpu.VMEM((RANGES, span, size, size), jnp.float32),
            pltpu.VMEM((RANGES, span, size, size), jnp.float32),
            pltpu.VMEM((places, size, DH), jnp.float32),
            pltpu.VMEM((places, size, DH), jnp.float32),
            pltpu.VMEM((RANGES, DH, size), jnp.float32),
            pltpu.VMEM((RANGES, DH, size), jnp.float32),
        ],
        compiler_params=pltpu.CompilerParams(vmem_limit_bytes=VMEM_BYTES),
        cost_estimate=pl.CostEstimate(
            flops=1, bytes_accessed=1, transcendentals=0
        ),
        name="attend",
    )(*operands)


def swap(value):
    return lax.all_to_all(value, GROUP, split_axis=0, concat_axis=0, tiled=True)


def shifted(value, steps):
    count = lax.axis_size("col")
    first, last = max(0, -steps), min(count, count - steps)
    return lax.ppermute(value, "col", [(at, at + steps) for at in range(first, last)])


def stamp_codes(audio_time):
    place = lax.axis_index("col") * RANGES + lax.axis_index("yh")
    code = jnp.where(audio_time >= 0, audio_time - place * SHARD_MS + 1, 0)
    pair = jnp.stack([code // STAMP_BASE, code % STAMP_BASE]).astype(jnp.bfloat16)
    return jnp.pad(pair, ((0, STAMP_ROWS - 2), (0, 0)))


def after(value, *others):
    return lax.optimization_barrier((value, others))[0]


def on_device(video_query, audio_key, audio_value, grad_out, audio_time):
    peers = lax.axis_size(GROUP)
    rows, width = video_query.shape
    heads = width // DH // peers
    early, late = CHUNKS
    key_plan = [(which, head) for head in early for which in (0, 1)]
    rest_plan = [(which, head) for head in early for which in (2, 3)]
    rest_plan += [(which, head) for head in late for which in (0, 1)]
    rest_plan += [(which, head) for head in late for which in (2, 3)]
    arrays = (audio_key, audio_value, video_query, grad_out)
    (key_pack,) = pack(arrays[:2], [key_plan], peers, stamp_codes(audio_time))
    own = swap(key_pack)
    left, right = shifted(own, 1), shifted(own, -1)
    (rest_pack,) = pack(arrays, [rest_plan], peers)
    rest = swap(after(rest_pack, own))
    late_rows = slice(2 * len(early) * rows, 2 * heads * rows)
    sent = after(rest[:, late_rows], left, right)
    late_left, late_right = shifted(sent, 1), shifted(sent, -1)

    def run(chunk, sides, firsts):
        return attend(
            chunk,
            (left, own, right),
            (rest, chunk[0] - firsts[0]),
            (sides, [chunk[0] - first for first in firsts[1:]]),
            (None, chunk[0]),
            ([None] * 3, chunk[0]),
            (len(chunk), len(chunk)),
        )

    def gather(sums, came):
        return sum(value.astype(jnp.float32) for value in (sums[1], *came)).astype(jnp.bfloat16)

    result, *sums = run(early, (left, own, right), (0, 0, 0, 0))
    to_left, to_right = after((sums[0], sums[2]), late_left, late_right)
    came = shifted(to_left, -1), shifted(to_right, 1)
    result = swap(result)
    last_result, *last_sums = run(late, (late_left, rest, late_right), (heads, 0, len(early), 0))
    to_left, to_right = after((last_sums[0], last_sums[2]), came)
    last_came = shifted(to_left, -1), shifted(to_right, 1)
    grads = swap(after(gather(sums, came), result))
    outs = place((result, grads), (0, 0), early, heads, rows, ())
    last = jnp.concatenate([last_result, gather(last_sums, last_came)], axis=1)
    last = swap(after(last, grads))
    offsets = (0, 2 * len(late) * rows)
    return tuple(place((last, last), offsets, late, heads, rows, outs))


def solution(mesh):
    columns = mesh.shape["seq"] // RANGES
    split = Mesh(
        mesh.devices.reshape(columns, RANGES, mesh.shape["head"]), ("col", "yh", "head")
    )
    rows = P(("col", "yh", "head"), None)
    return jax.shard_map(
        on_device,
        mesh=split,
        in_specs=(rows, rows, rows, rows, P(("col", "yh", "head"))),
        out_specs=(rows, rows, rows, rows),
        check_vma=False,
    )
```

```python
import functools
import math

import jax
import jax.numpy as jnp
from jax import lax
from jax.experimental import pallas as pl
from jax.experimental.pallas import tpu as pltpu
from jax.sharding import Mesh
from jax.sharding import PartitionSpec as P

DH = 128
SHARD_MS = 625
RADIUS_MS = 1000
NEG_FILL = -1e30
FAR = -1e6
SCALE = DH ** (-0.5)
LOG2E = 1.4426950408889634
GROUP = ("yh", "head")
CHUNKS = ((0,), (1, 2))
STAMP_ROWS = 16
STAMP_BASE = 32
RANGES = 2
UNROLL = True
REACH = 2
VMEM_BYTES = 56 * 1024 * 1024


def dot(lhs, rhs, dims):
    return lax.dot_general(lhs, rhs, (dims, ((), ())), preferred_element_type=jnp.float32)


def dot_nn(lhs, rhs):
    return dot(lhs, rhs, ((1,), (0,)))


def dot_nt(lhs, rhs):
    return dot(lhs, rhs, ((1,), (1,)))


def pack_kernel(peers, heads, plans, stamped, count, *refs):
    ins, outs = refs[:count], refs[count + stamped :]
    rows = ins[0].shape[0]
    for number, (out, plan) in enumerate(zip(outs, plans)):
        for peer in range(peers):
            for at, (which, head) in enumerate(plan):
                lanes = pl.ds((peer * heads + head) * DH, DH)
                out[peer, pl.ds(at * rows, rows)] = ins[which][:, lanes]
    if stamped:
        stamp = refs[count][...]
        place = lax.axis_index("col") * RANGES + lax.axis_index("yh")
        code = jnp.where(stamp >= 0, stamp - place * SHARD_MS + 1, 0)
        row = lax.broadcasted_iota(jnp.int32, (STAMP_ROWS, rows), 0)
        code = jnp.broadcast_to(code, (STAMP_ROWS, rows))
        code = jnp.where(row == 0, code // STAMP_BASE, code % STAMP_BASE)
        code = code.astype(jnp.float32).astype(jnp.bfloat16)
        for peer in range(peers):
            outs[0][peer, pl.ds(len(plans[0]) * rows, STAMP_ROWS)] = code


def pack(arrays, plans, peers, stamp_rows=None):
    rows, width = arrays[0].shape
    stamps = [] if stamp_rows is None else [stamp_rows.reshape(1, rows)]
    extra = [STAMP_ROWS if stamps and number == 0 else 0 for number in range(len(plans))]
    return pl.pallas_call(
        functools.partial(
            pack_kernel, peers, width // DH // peers, plans, len(stamps), len(arrays)
        ),
        out_shape=[
            jax.ShapeDtypeStruct((peers, len(plan) * rows + more, DH), arrays[0].dtype)
            for plan, more in zip(plans, extra)
        ],
        compiler_params=pltpu.CompilerParams(vmem_limit_bytes=VMEM_BYTES),
        name="pack",
    )(*arrays, *stamps)


def place_kernel(peers, heads, chunk, offset, piece, *refs):
    outs, sems = refs[-3:-1], refs[-1]
    rows = outs[0].shape[0]
    copies = []
    for peer in range(peers):
        for place, head in enumerate(chunk):
            lanes = pl.ds((peer * heads + head) * DH, DH)
            for which, out in enumerate(outs):
                start = offset + (2 * place + which) * rows
                copies.append(
                    pltpu.make_async_copy(
                        piece.at[peer, pl.ds(start, rows)],
                        out.at[:, lanes],
                        sems.at[len(copies)],
                    )
                )
    for copy in copies:
        copy.start()
    for copy in copies:
        copy.wait()


def place(piece, offset, chunk, heads, rows, outs=()):
    peers = piece.shape[0]
    shape = jax.ShapeDtypeStruct((rows, peers * heads * DH), piece.dtype)
    anywhere = pl.BlockSpec(memory_space=pl.ANY)
    return pl.pallas_call(
        functools.partial(place_kernel, peers, heads, chunk, offset),
        in_specs=[pl.BlockSpec(memory_space=pltpu.VMEM)] + [anywhere] * len(outs),
        out_specs=[anywhere] * 2,
        out_shape=[shape] * 2,
        input_output_aliases={1 + at: at for at in range(len(outs))},
        scratch_shapes=[pltpu.SemaphoreType.DMA((2 * peers * len(chunk),))],
        compiler_params=pltpu.CompilerParams(vmem_limit_bytes=VMEM_BYTES),
        name="place",
    )(piece, *outs)


def spread_stamps(codes, shift):
    size = codes.shape[1]
    place = lax.broadcasted_iota(jnp.int32, (size, size), 0)
    diagonal = place == lax.broadcasted_iota(jnp.int32, (size, size), 1)
    ones = jnp.ones((size, size), jnp.bfloat16)
    found = [
        dot_nn(jnp.where(diagonal, codes[row : row + 1].astype(jnp.float32), 0.0).astype(jnp.bfloat16), ones)
        for row in range(2)
    ]
    code = found[0] * STAMP_BASE + found[1]
    return jnp.where(code > 0.5, code + (shift - 1), FAR)


def attend_kernel(
    per, size, fresh,
    stamps_left, stamps_own, stamps_right, qg_ref, left_ref, own_ref, right_ref, *refs
):
    skip = 4 - sum(fresh)
    result_ref, to_left_ref, own_sum_ref, to_right_ref = refs[skip : skip + 4]
    (
        stamps,
        scores, key_sums, value_sums, total_t, query_t,
    ) = refs[skip + 4 :]
    rows = size // per
    span = 2 * REACH + 1

    @pl.when(pl.program_id(0) == 0)
    def _():
        for side, ref in enumerate((stamps_left, stamps_own, stamps_right)):
            for block in range(RANGES * per):
                place = side * RANGES + block // per
                spread = spread_stamps(ref[block], (place - RANGES) * SHARD_MS)
                stamps[place, pl.ds(block % per * rows, rows)] = spread

    def slots(place, which):
        ref = (left_ref, own_ref, right_ref)[place // RANGES]
        found = ref[pl.ds(place % RANGES * per, per), pl.ds(which * rows, rows)]
        return found.reshape(size, DH)

    keys = [slots(place, 0) for place in range(3 * RANGES)]
    values = [slots(place, 1) for place in range(3 * RANGES)]
    offsets = lax.broadcasted_iota(jnp.int32, (1, size), 1) * SHARD_MS // size
    blocks = [pl.ds(part * per, per) for part in range(RANGES)]
    query = [qg_ref[block, pl.ds(0, rows)].reshape(size, DH) for block in blocks]
    grad = [qg_ref[block, pl.ds(rows, rows)].reshape(size, DH) for block in blocks]
    stamp = [(offsets + part * SHARD_MS).astype(jnp.float32) for part in range(RANGES)]
    top, inverse, row_dot = [None] * RANGES, [None] * RANGES, [None] * RANGES

    def add(ref, at, fresh, value):
        ref[at] = value if fresh else ref[at] + value

    def unrolled(body, carry):
        for step in range(span):
            carry = body(step, carry)
        return carry

    def score_step(part, step, top):
        place = step + part
        found = dot_nt(keys[place], query[part])
        near = jnp.abs(jnp.tile(stamps[place], (1, size // DH)) - stamp[part]) <= RADIUS_MS
        found = jnp.where(near, found * (SCALE * LOG2E), NEG_FILL)
        scores[part, step] = found
        return jnp.maximum(top, jnp.max(found.reshape(size // 8, 8, size), axis=0))

    def weight_step(part, step, total):
        place = step + part
        raised = jnp.exp2(scores[part, step] - top[part])
        scores[part, step] = raised
        add(total_t, part, step == 0, dot(values[place], raised.astype(jnp.bfloat16), ((0,), (0,))))
        return total + jnp.sum(raised.reshape(size // 8, 8, size), axis=0)

    def grad_step(part, step):
        place = step + part
        weights = scores[part, step] * inverse[part]
        slopes = (weights * (dot_nt(values[place], grad[part]) - row_dot[part])).astype(jnp.bfloat16)
        fresh = part == 0 or step == span - 1
        add(value_sums, place, fresh, dot_nn(weights.astype(jnp.bfloat16), grad[part]))
        add(key_sums, place, fresh, dot_nn(slopes, query[part]))
        add(query_t, part, step == 0, dot(keys[place], slopes, ((0,), (0,))))

    def finish(part, total):
        inverse[part] = 1.0 / jnp.sum(total, axis=0, keepdims=True)
        attended_t = total_t[part] * inverse[part]
        row_dot[part] = jnp.sum(
            attended_t * grad[part].astype(jnp.float32).T, axis=0, keepdims=True
        )
        shape = (per, rows, DH)
        result_ref[blocks[part], pl.ds(0, rows)] = attended_t.T.astype(jnp.bfloat16).reshape(shape)

    def finish_query(part):
        low = (query_t[part] * SCALE).T.astype(jnp.bfloat16)
        result_ref[blocks[part], pl.ds(rows, rows)] = low.reshape(per, rows, DH)

    lowest = jnp.full((8, size), NEG_FILL, jnp.float32)
    zero = jnp.zeros((8, size), jnp.float32)
    found = unrolled(lambda step, c: score_step(0, step, c), lowest)
    top[0] = jnp.max(found, axis=0, keepdims=True)

    def second(step, carry):
        return weight_step(0, step, carry[0]), score_step(1, step, carry[1])

    total, found = unrolled(second, (zero, lowest))
    top[1] = jnp.max(found, axis=0, keepdims=True)
    finish(0, total)

    def third(step, carry):
        grad_step(0, step)
        return weight_step(1, step, carry)

    total = unrolled(third, zero)
    finish_query(0)
    finish(1, total)

    def fourth(step, carry):
        grad_step(1, step)
        return carry

    unrolled(fourth, 0)
    finish_query(1)
    for side, ref in enumerate((to_left_ref, own_sum_ref, to_right_ref)):
        for part in range(RANGES):
            place = side * RANGES + part
            shape = (per, rows, DH)
            ref[blocks[part], pl.ds(0, rows)] = (key_sums[place] * SCALE).astype(ref.dtype).reshape(shape)
            ref[blocks[part], pl.ds(rows, rows)] = value_sums[place].astype(ref.dtype).reshape(shape)


def attend(heads, stamped, query_grad, sides, result, sums, sizes):
    peers = stamped[0].shape[0]
    per = peers // RANGES
    rows = (stamped[0].shape[1] - STAMP_ROWS) // (2 * len(CHUNKS[0]))
    size = per * rows
    span = 2 * REACH + 1
    places = 3 * RANGES

    def piece(first):
        start = heads[0] - first
        return pl.BlockSpec((peers, 2 * rows, DH), lambda head: (0, start + head, 0))

    stamp_block = 2 * len(CHUNKS[0]) * rows // STAMP_ROWS
    stamp_spec = pl.BlockSpec((peers, STAMP_ROWS, DH), lambda head: (0, stamp_block, 0))
    old = [result[0], *sums[0]]
    firsts = [result[1]] + [sums[1]] * 3
    kinds = [jnp.bfloat16] * 4
    counts = [sizes[0]] + [sizes[1]] * 3
    fresh = [value is None for value in old]
    operands = [*stamped, query_grad[0], *sides[0]]
    in_specs = [stamp_spec] * 3 + [piece(first) for first in (query_grad[1], *sides[1])]
    aliases = {}
    for number, value in enumerate(old):
        if value is not None:
            aliases[len(operands)] = number
            operands.append(value)
            in_specs.append(pl.BlockSpec(memory_space=pl.ANY))

    return pl.pallas_call(
        functools.partial(attend_kernel, per, size, fresh),
        grid=(len(heads),),
        in_specs=in_specs,
        out_specs=[piece(first) for first in firsts],
        out_shape=[
            jax.ShapeDtypeStruct((peers, 2 * rows * count, DH), kind)
            for count, kind in zip(counts, kinds)
        ],
        input_output_aliases=aliases,
        scratch_shapes=[
            pltpu.VMEM((places, size, DH), jnp.float32),
            pltpu.VMEM((RANGES, span, size, size), jnp.float32),
            pltpu.VMEM((places, size, DH), jnp.float32),
            pltpu.VMEM((places, size, DH), jnp.float32),
            pltpu.VMEM((RANGES, DH, size), jnp.float32),
            pltpu.VMEM((RANGES, DH, size), jnp.float32),
        ],
        compiler_params=pltpu.CompilerParams(vmem_limit_bytes=VMEM_BYTES),
        cost_estimate=pl.CostEstimate(
            flops=1, bytes_accessed=1, transcendentals=0
        ),
        name="attend",
    )(*operands)


def swap(value):
    return lax.all_to_all(value, GROUP, split_axis=0, concat_axis=0, tiled=True)


def shifted(value, steps):
    count = lax.axis_size("col")
    first, last = max(0, -steps), min(count, count - steps)
    return lax.ppermute(value, "col", [(at, at + steps) for at in range(first, last)])


def after(value, *others):
    return lax.optimization_barrier((value, others))[0]


def on_device(video_query, audio_key, audio_value, grad_out, audio_time):
    peers = lax.axis_size(GROUP)
    rows, width = video_query.shape
    heads = width // DH // peers
    early, late = CHUNKS
    block = 2 * rows
    arrays = (audio_key, audio_value, video_query, grad_out)
    key_plan = [(which, head) for head in early for which in (0, 1)]
    mixed_plan = [(which, head) for head in early for which in (2, 3)]
    mixed_plan += [(which, head) for head in late for which in (0, 1)]
    query_plan = [(which, head) for head in late for which in (2, 3)]
    (key_pack,) = pack(arrays[:2], [key_plan], peers, audio_time)
    own = swap(key_pack)
    mixed_pack, query_pack = pack(arrays, [mixed_plan, query_plan], peers)
    mixed = swap(after(mixed_pack, own))
    left, right = shifted(own, 1), shifted(own, -1)
    sent = after(mixed[:, block * len(early) :], left, right)
    late_left, late_right = shifted(sent, 1), shifted(sent, -1)
    queries = swap(after(query_pack, mixed))

    def gather(sums, came):
        return sum(value.astype(jnp.float32) for value in (sums[1], *came)).astype(jnp.bfloat16)

    stamped = (left, own, right)
    result, *sums = attend(
        early, stamped, (mixed, 0), (stamped, (0, 0, 0)), (None, 0), ([None] * 3, 0),
        (heads + len(early), len(early)),
    )
    came = shifted(sums[0], -1), shifted(sums[2], 1)
    first = late[0]
    result, *late_sums = attend(
        late, stamped, (queries, first), ((late_left, mixed, late_right), (first, 0, first)),
        (result, 0), ([None] * 3, first), (heads + len(early), len(late)),
    )
    to_left, to_right = after((late_sums[0], late_sums[2]), came)
    late_came = shifted(to_left, -1), shifted(to_right, 1)
    result = lax.dynamic_update_slice(result, gather(sums, came), (0, block * heads, 0))
    result = swap(result)
    grads = swap(gather(late_sums, late_came))
    attended = place(result, 0, early + late, heads, rows)
    grad = place(result, block * heads, early, heads, rows)
    return (*attended, *place(grads, 0, late, heads, rows, grad))


def solution(mesh):
    columns = mesh.shape["seq"] // RANGES
    split = Mesh(
        mesh.devices.reshape(columns, RANGES, mesh.shape["head"]), ("col", "yh", "head")
    )
    rows = P(("col", "yh", "head"), None)
    return jax.shard_map(
        on_device,
        mesh=split,
        in_specs=(rows, rows, rows, rows, P(("col", "yh", "head"))),
        out_specs=(rows, rows, rows, rows),
        check_vma=False,
    )
```

```python
import functools
import math

import jax
import jax.numpy as jnp
from jax import lax
from jax.experimental import pallas as pl
from jax.experimental.pallas import tpu as pltpu
from jax.sharding import Mesh
from jax.sharding import PartitionSpec as P

DH = 128
SHARD_MS = 625
RADIUS_MS = 1000
NEG_FILL = -1e30
FAR = -1e6
SCALE = DH ** (-0.5)
LOG2E = 1.4426950408889634
GROUP = ("yh", "head")
CHUNKS = ((0,), (1, 2))
STAMP_ROWS = 16
STAMP_BASE = 32
RANGES = 2
TILE = 2560
REACH = 2
VMEM_BYTES = 56 * 1024 * 1024
PLACE_BYTES = 8 * 1024 * 1024


def dot(lhs, rhs, dims):
    return lax.dot_general(lhs, rhs, (dims, ((), ())), preferred_element_type=jnp.float32)


def dot_nn(lhs, rhs):
    return dot(lhs, rhs, ((1,), (0,)))


def dot_nt(lhs, rhs):
    return dot(lhs, rhs, ((1,), (1,)))


def pack_kernel(peers, heads, plans, stamped, count, *refs):
    ins, outs = refs[:count], refs[count + stamped :]
    rows = ins[0].shape[0]
    for number, (out, plan) in enumerate(zip(outs, plans)):
        for peer in range(peers):
            for at, (which, head) in enumerate(plan):
                lanes = pl.ds((peer * heads + head) * DH, DH)
                out[peer, pl.ds(at * rows, rows)] = ins[which][:, lanes]
    if stamped:
        stamp = refs[count][...]
        place = lax.axis_index("col") * RANGES + lax.axis_index("yh")
        code = jnp.where(stamp >= 0, stamp - place * SHARD_MS + 1, 0)
        row = lax.broadcasted_iota(jnp.int32, (STAMP_ROWS, rows), 0)
        code = jnp.broadcast_to(code, (STAMP_ROWS, rows))
        code = jnp.where(row == 0, code // STAMP_BASE, code % STAMP_BASE)
        code = code.astype(jnp.float32).astype(jnp.bfloat16)
        for peer in range(peers):
            outs[0][peer, pl.ds(len(plans[0]) * rows, STAMP_ROWS)] = code


def pack(arrays, plans, peers, stamp_rows=None):
    rows, width = arrays[0].shape
    stamps = [] if stamp_rows is None else [stamp_rows.reshape(1, rows)]
    extra = [STAMP_ROWS if stamps and number == 0 else 0 for number in range(len(plans))]
    return pl.pallas_call(
        functools.partial(
            pack_kernel, peers, width // DH // peers, plans, len(stamps), len(arrays)
        ),
        out_shape=[
            jax.ShapeDtypeStruct((peers, len(plan) * rows + more, DH), arrays[0].dtype)
            for plan, more in zip(plans, extra)
        ],
        compiler_params=pltpu.CompilerParams(vmem_limit_bytes=VMEM_BYTES),
        name="pack",
    )(*arrays, *stamps)


def place_kernel(peers, heads, chunk, offset, piece, *refs):
    outs, sems = refs[-3:-1], refs[-1]
    rows = outs[0].shape[0]
    copies = []
    for peer in range(peers):
        for place, head in enumerate(chunk):
            lanes = pl.ds((peer * heads + head) * DH, DH)
            for which, out in enumerate(outs):
                start = offset + (2 * place + which) * rows
                copies.append(
                    pltpu.make_async_copy(
                        piece.at[peer, pl.ds(start, rows)],
                        out.at[:, lanes],
                        sems.at[len(copies)],
                    )
                )
    for copy in copies:
        copy.start()
    for copy in copies:
        copy.wait()


def place(piece, offset, chunk, heads, rows, outs=()):
    peers = piece.shape[0]
    shape = jax.ShapeDtypeStruct((rows, peers * heads * DH), piece.dtype)
    anywhere = pl.BlockSpec(memory_space=pl.ANY)
    return pl.pallas_call(
        functools.partial(place_kernel, peers, heads, chunk, offset),
        in_specs=[pl.BlockSpec(memory_space=pltpu.VMEM)] + [anywhere] * len(outs),
        out_specs=[anywhere] * 2,
        out_shape=[shape] * 2,
        input_output_aliases={1 + at: at for at in range(len(outs))},
        scratch_shapes=[pltpu.SemaphoreType.DMA((2 * peers * len(chunk),))],
        compiler_params=pltpu.CompilerParams(vmem_limit_bytes=PLACE_BYTES),
        name="place",
    )(piece, *outs)


def spread_stamps(codes, shift):
    size = codes.shape[1]
    place = lax.broadcasted_iota(jnp.int32, (size, size), 0)
    diagonal = place == lax.broadcasted_iota(jnp.int32, (size, size), 1)
    ones = jnp.ones((size, size), jnp.bfloat16)
    found = [
        dot_nn(jnp.where(diagonal, codes[row : row + 1].astype(jnp.float32), 0.0).astype(jnp.bfloat16), ones)
        for row in range(2)
    ]
    code = found[0] * STAMP_BASE + found[1]
    return jnp.where(code > 0.5, code + (shift - 1), FAR)


def attend_kernel(
    per, size, fresh,
    stamps_left, stamps_own, stamps_right, qg_ref, left_ref, own_ref, right_ref, *refs
):
    skip = 4 - sum(fresh)
    result_ref, to_left_ref, own_sum_ref, to_right_ref = refs[skip : skip + 4]
    (
        stamps, keys, values,
        scores, key_sums, value_sums, total_t, query_t,
    ) = refs[skip + 4 :]
    rows = size // per
    span = (2 * REACH + 1) * size // TILE

    @pl.when(pl.program_id(0) == 0)
    def _():
        for side, ref in enumerate((stamps_left, stamps_own, stamps_right)):
            for block in range(RANGES * per):
                place = side * RANGES * per + block
                spread = spread_stamps(ref[block], (place // per - RANGES) * SHARD_MS)
                stamps[pl.ds(place * rows, rows)] = spread

    for place in range(3 * RANGES):
        ref = (left_ref, own_ref, right_ref)[place // RANGES]
        part = pl.ds(place % RANGES * per, per)
        keys[pl.ds(place * size, size)] = ref[part, pl.ds(0, rows)].reshape(size, DH)
        values[pl.ds(place * size, size)] = ref[part, pl.ds(rows, rows)].reshape(size, DH)
    tail = pl.ds((2 * REACH + 1) * size, size)
    key_sums[tail] = jnp.zeros((size, DH), jnp.float32)
    value_sums[tail] = jnp.zeros((size, DH), jnp.float32)
    offsets = lax.broadcasted_iota(jnp.int32, (1, size), 1) * SHARD_MS // size
    blocks = [pl.ds(part * per, per) for part in range(RANGES)]
    query = [qg_ref[block, pl.ds(0, rows)].reshape(size, DH) for block in blocks]
    grad = [qg_ref[block, pl.ds(rows, rows)].reshape(size, DH) for block in blocks]
    stamp = [(offsets + part * SHARD_MS).astype(jnp.float32) for part in range(RANGES)]
    top, inverse, row_dot = [None] * RANGES, [None] * RANGES, [None] * RANGES

    def add(ref, at, fresh, value):
        ref[at] = value if fresh else ref[at] + value

    def unrolled(body, carry):
        for step in range(span):
            carry = body(step, carry)
        return carry

    def score_step(part, step, top):
        place = pl.ds(part * size + step * TILE, TILE)
        found = dot_nt(keys[place], query[part])
        near = jnp.abs(jnp.tile(stamps[place], (1, size // DH)) - stamp[part]) <= RADIUS_MS
        found = jnp.where(near, found * (SCALE * LOG2E), NEG_FILL)
        scores[part, step] = found
        return jnp.maximum(top, jnp.max(found.reshape(TILE // 8, 8, size), axis=0))

    def weight_step(part, step, total):
        place = pl.ds(part * size + step * TILE, TILE)
        raised = jnp.exp2(scores[part, step] - top[part])
        scores[part, step] = raised
        add(total_t, part, step == 0, dot(values[place], raised.astype(jnp.bfloat16), ((0,), (0,))))
        return total + jnp.sum(raised.reshape(TILE // 8, 8, size), axis=0)

    def grad_step(part, step):
        place = pl.ds(part * size + step * TILE, TILE)
        weights = scores[part, step] * inverse[part]
        slopes = (weights * (dot_nt(values[place], grad[part]) - row_dot[part])).astype(jnp.bfloat16)
        fresh = part == 0
        add(value_sums, place, fresh, dot_nn(weights.astype(jnp.bfloat16), grad[part]))
        add(key_sums, place, fresh, dot_nn(slopes, query[part]))
        add(query_t, part, step == 0, dot(keys[place], slopes, ((0,), (0,))))

    def finish(part, total):
        inverse[part] = 1.0 / jnp.sum(total, axis=0, keepdims=True)
        attended_t = total_t[part] * inverse[part]
        row_dot[part] = jnp.sum(
            attended_t * grad[part].astype(jnp.float32).T, axis=0, keepdims=True
        )
        shape = (per, rows, DH)
        result_ref[blocks[part], pl.ds(0, rows)] = attended_t.T.astype(jnp.bfloat16).reshape(shape)

    def finish_query(part):
        low = (query_t[part] * SCALE).T.astype(jnp.bfloat16)
        result_ref[blocks[part], pl.ds(rows, rows)] = low.reshape(per, rows, DH)

    lowest = jnp.full((8, size), NEG_FILL, jnp.float32)
    zero = jnp.zeros((8, size), jnp.float32)
    found = unrolled(lambda step, c: score_step(0, step, c), lowest)
    top[0] = jnp.max(found, axis=0, keepdims=True)

    def second(step, carry):
        return weight_step(0, step, carry[0]), score_step(1, step, carry[1])

    total, found = unrolled(second, (zero, lowest))
    top[1] = jnp.max(found, axis=0, keepdims=True)
    finish(0, total)

    def third(step, carry):
        grad_step(0, step)
        return weight_step(1, step, carry)

    total = unrolled(third, zero)
    finish_query(0)
    finish(1, total)

    def fourth(step, carry):
        grad_step(1, step)
        return carry

    unrolled(fourth, 0)
    finish_query(1)
    for side, ref in enumerate((to_left_ref, own_sum_ref, to_right_ref)):
        for part in range(RANGES):
            place = pl.ds((side * RANGES + part) * size, size)
            shape = (per, rows, DH)
            ref[blocks[part], pl.ds(0, rows)] = (key_sums[place] * SCALE).astype(ref.dtype).reshape(shape)
            ref[blocks[part], pl.ds(rows, rows)] = value_sums[place].astype(ref.dtype).reshape(shape)


def attend(heads, stamped, query_grad, sides, result, sums, sizes):
    peers = stamped[0].shape[0]
    per = peers // RANGES
    rows = (stamped[0].shape[1] - STAMP_ROWS) // (2 * len(CHUNKS[0]))
    size = per * rows
    span = 2 * REACH + 1
    places = 3 * RANGES

    def piece(first):
        start = heads[0] - first
        return pl.BlockSpec((peers, 2 * rows, DH), lambda head: (0, start + head, 0))

    stamp_block = 2 * len(CHUNKS[0]) * rows // STAMP_ROWS
    stamp_spec = pl.BlockSpec((peers, STAMP_ROWS, DH), lambda head: (0, stamp_block, 0))
    old = [result[0], *sums[0]]
    firsts = [result[1]] + [sums[1]] * 3
    kinds = [jnp.bfloat16] * 4
    counts = [sizes[0]] + [sizes[1]] * 3
    fresh = [value is None for value in old]
    operands = [*stamped, query_grad[0], *sides[0]]
    in_specs = [stamp_spec] * 3 + [piece(first) for first in (query_grad[1], *sides[1])]
    aliases = {}
    for number, value in enumerate(old):
        if value is not None:
            aliases[len(operands)] = number
            operands.append(value)
            in_specs.append(pl.BlockSpec(memory_space=pl.ANY))

    return pl.pallas_call(
        functools.partial(attend_kernel, per, size, fresh),
        grid=(len(heads),),
        in_specs=in_specs,
        out_specs=[piece(first) for first in firsts],
        out_shape=[
            jax.ShapeDtypeStruct((peers, 2 * rows * count, DH), kind)
            for count, kind in zip(counts, kinds)
        ],
        input_output_aliases=aliases,
        scratch_shapes=[
            pltpu.VMEM((places * size, DH), jnp.float32),
            pltpu.VMEM((places * size, DH), jnp.bfloat16),
            pltpu.VMEM((places * size, DH), jnp.bfloat16),
            pltpu.VMEM((RANGES, span * size // TILE, TILE, size), jnp.float32),
            pltpu.VMEM((places * size, DH), jnp.float32),
            pltpu.VMEM((places * size, DH), jnp.float32),
            pltpu.VMEM((RANGES, DH, size), jnp.float32),
            pltpu.VMEM((RANGES, DH, size), jnp.float32),
        ],
        compiler_params=pltpu.CompilerParams(vmem_limit_bytes=VMEM_BYTES),
        cost_estimate=pl.CostEstimate(
            flops=1, bytes_accessed=1, transcendentals=0
        ),
        name="attend",
    )(*operands)


def swap(value):
    return lax.all_to_all(value, GROUP, split_axis=0, concat_axis=0, tiled=True)


def shifted(value, steps):
    count = lax.axis_size("col")
    first, last = max(0, -steps), min(count, count - steps)
    return lax.ppermute(value, "col", [(at, at + steps) for at in range(first, last)])


def after(value, *others):
    return lax.optimization_barrier((value, others))[0]


def on_device(video_query, audio_key, audio_value, grad_out, audio_time):
    peers = lax.axis_size(GROUP)
    rows, width = video_query.shape
    heads = width // DH // peers
    early, late = CHUNKS
    block = 2 * rows
    arrays = (audio_key, audio_value, video_query, grad_out)
    key_plan = [(which, head) for head in early for which in (0, 1)]
    mixed_plan = [(which, head) for head in early for which in (2, 3)]
    mixed_plan += [(which, head) for head in late for which in (0, 1)]
    query_plan = [(which, head) for head in late for which in (2, 3)]
    (key_pack,) = pack(arrays[:2], [key_plan], peers, audio_time)
    own = swap(key_pack)
    mixed_pack, query_pack = pack(arrays, [mixed_plan, query_plan], peers)
    mixed = swap(after(mixed_pack, own))
    left, right = shifted(own, 1), shifted(own, -1)
    sent = after(mixed[:, block * len(early) :], left, right)
    late_left, late_right = shifted(sent, 1), shifted(sent, -1)
    queries = swap(after(query_pack, mixed))

    def gather(sums, came):
        return sum(value.astype(jnp.float32) for value in (sums[1], *came)).astype(jnp.bfloat16)

    stamped = (left, own, right)
    result, *sums = attend(
        early, stamped, (mixed, 0), (stamped, (0, 0, 0)), (None, 0), ([None] * 3, 0),
        (heads + len(early), len(early)),
    )
    came = shifted(sums[0], -1), shifted(sums[2], 1)
    first = late[0]
    result, *late_sums = attend(
        late, stamped, (queries, first), ((late_left, mixed, late_right), (first, 0, first)),
        (result, 0), ([None] * 3, first), (heads + len(early), len(late)),
    )
    to_left, to_right = after((late_sums[0], late_sums[2]), came)
    late_came = shifted(to_left, -1), shifted(to_right, 1)
    result = lax.dynamic_update_slice(result, gather(sums, came), (0, block * heads, 0))
    result = swap(result)
    grads = swap(gather(late_sums, late_came))
    attended = place(result, 0, early + late, heads, rows)
    grad = place(result, block * heads, early, heads, rows)
    return (*attended, *place(grads, 0, late, heads, rows, grad))


def solution(mesh):
    columns = mesh.shape["seq"] // RANGES
    split = Mesh(
        mesh.devices.reshape(columns, RANGES, mesh.shape["head"]), ("col", "yh", "head")
    )
    rows = P(("col", "yh", "head"), None)
    return jax.shard_map(
        on_device,
        mesh=split,
        in_specs=(rows, rows, rows, rows, P(("col", "yh", "head"))),
        out_specs=(rows, rows, rows, rows),
        check_vma=False,
    )
```

```python
import functools
import math

import jax
import jax.numpy as jnp
from jax import lax
from jax.experimental import pallas as pl
from jax.experimental.pallas import tpu as pltpu
from jax.sharding import Mesh
from jax.sharding import PartitionSpec as P

DH = 128
SHARD_MS = 625
RADIUS_MS = 1000
NEG_FILL = -1e30
FAR = -1e6
SCALE = DH ** (-0.5)
LOG2E = 1.4426950408889634
GROUP = ("yh", "head")
CHUNKS = ((0,), (1, 2))
STAMP_ROWS = 16
STAMP_BASE = 32
RANGES = 2
TILE = 2560
REACH = 2
VMEM_BYTES = 56 * 1024 * 1024
PLACE_BYTES = 8 * 1024 * 1024
PACK_BYTES = 12 * 1024 * 1024


def dot(lhs, rhs, dims):
    return lax.dot_general(lhs, rhs, (dims, ((), ())), preferred_element_type=jnp.float32)


def dot_nn(lhs, rhs):
    return dot(lhs, rhs, ((1,), (0,)))


def dot_nt(lhs, rhs):
    return dot(lhs, rhs, ((1,), (1,)))


def pack_kernel(peers, heads, plans, stamped, count, *refs):
    ins, outs = refs[:count], refs[count + stamped :]
    rows = ins[0].shape[0]
    for number, (out, plan) in enumerate(zip(outs, plans)):
        for peer in range(peers):
            for at, (which, head) in enumerate(plan):
                lanes = pl.ds((peer * heads + head) * DH, DH)
                out[peer, pl.ds(at * rows, rows)] = ins[which][:, lanes]
    if stamped:
        stamp = refs[count][...]
        place = lax.axis_index("col") * RANGES + lax.axis_index("yh")
        code = jnp.where(stamp >= 0, stamp - place * SHARD_MS + 1, 0)
        row = lax.broadcasted_iota(jnp.int32, (STAMP_ROWS, rows), 0)
        code = jnp.broadcast_to(code, (STAMP_ROWS, rows))
        code = jnp.where(row == 0, code // STAMP_BASE, code % STAMP_BASE)
        code = code.astype(jnp.float32).astype(jnp.bfloat16)
        for peer in range(peers):
            outs[0][peer, pl.ds(len(plans[0]) * rows, STAMP_ROWS)] = code


def pack(arrays, plans, peers, stamp_rows=None):
    rows, width = arrays[0].shape
    stamps = [] if stamp_rows is None else [stamp_rows.reshape(1, rows)]
    extra = [STAMP_ROWS if stamps and number == 0 else 0 for number in range(len(plans))]
    return pl.pallas_call(
        functools.partial(
            pack_kernel, peers, width // DH // peers, plans, len(stamps), len(arrays)
        ),
        out_shape=[
            jax.ShapeDtypeStruct((peers, len(plan) * rows + more, DH), arrays[0].dtype)
            for plan, more in zip(plans, extra)
        ],
        compiler_params=pltpu.CompilerParams(vmem_limit_bytes=PACK_BYTES),
        name="pack",
    )(*arrays, *stamps)


def place_kernel(peers, heads, chunk, offset, piece, *refs):
    outs, sems = refs[-3:-1], refs[-1]
    rows = outs[0].shape[0]
    copies = []
    for peer in range(peers):
        for place, head in enumerate(chunk):
            lanes = pl.ds((peer * heads + head) * DH, DH)
            for which, out in enumerate(outs):
                start = offset + (2 * place + which) * rows
                copies.append(
                    pltpu.make_async_copy(
                        piece.at[peer, pl.ds(start, rows)],
                        out.at[:, lanes],
                        sems.at[len(copies)],
                    )
                )
    for copy in copies:
        copy.start()
    for copy in copies:
        copy.wait()


def place(piece, offset, chunk, heads, rows, outs=()):
    peers = piece.shape[0]
    shape = jax.ShapeDtypeStruct((rows, peers * heads * DH), piece.dtype)
    anywhere = pl.BlockSpec(memory_space=pl.ANY)
    return pl.pallas_call(
        functools.partial(place_kernel, peers, heads, chunk, offset),
        in_specs=[pl.BlockSpec(memory_space=pltpu.VMEM)] + [anywhere] * len(outs),
        out_specs=[anywhere] * 2,
        out_shape=[shape] * 2,
        input_output_aliases={1 + at: at for at in range(len(outs))},
        scratch_shapes=[pltpu.SemaphoreType.DMA((2 * peers * len(chunk),))],
        compiler_params=pltpu.CompilerParams(vmem_limit_bytes=PLACE_BYTES),
        name="place",
    )(piece, *outs)


def spread_stamps(codes, shift):
    size = codes.shape[1]
    place = lax.broadcasted_iota(jnp.int32, (size, size), 0)
    diagonal = place == lax.broadcasted_iota(jnp.int32, (size, size), 1)
    ones = jnp.ones((size, size), jnp.bfloat16)
    found = [
        dot_nn(jnp.where(diagonal, codes[row : row + 1].astype(jnp.float32), 0.0).astype(jnp.bfloat16), ones)
        for row in range(2)
    ]
    code = found[0] * STAMP_BASE + found[1]
    return jnp.where(code > 0.5, code + (shift - 1), FAR)


def attend_kernel(
    per, size, fresh,
    stamps_left, stamps_own, stamps_right, qg_ref, left_ref, own_ref, right_ref, *refs
):
    skip = 4 - sum(fresh)
    result_ref, to_left_ref, own_sum_ref, to_right_ref = refs[skip : skip + 4]
    (
        stamps, keys, values,
        scores, key_sums, value_sums, total_t, query_t,
    ) = refs[skip + 4 :]
    rows = size // per
    span = (2 * REACH + 1) * size // TILE

    @pl.when(pl.program_id(0) == 0)
    def _():
        for side, ref in enumerate((stamps_left, stamps_own, stamps_right)):
            for block in range(RANGES * per):
                place = side * RANGES * per + block
                spread = spread_stamps(ref[block], (place // per - RANGES) * SHARD_MS)
                stamps[pl.ds(place * rows, rows)] = spread

    for place in range(3 * RANGES):
        ref = (left_ref, own_ref, right_ref)[place // RANGES]
        part = pl.ds(place % RANGES * per, per)
        keys[pl.ds(place * size, size)] = ref[part, pl.ds(0, rows)].reshape(size, DH)
        values[pl.ds(place * size, size)] = ref[part, pl.ds(rows, rows)].reshape(size, DH)
    tail = pl.ds((2 * REACH + 1) * size, size)
    key_sums[tail] = jnp.zeros((size, DH), jnp.float32)
    value_sums[tail] = jnp.zeros((size, DH), jnp.float32)
    offsets = lax.broadcasted_iota(jnp.int32, (1, size), 1) * SHARD_MS // size
    blocks = [pl.ds(part * per, per) for part in range(RANGES)]
    query = [qg_ref[block, pl.ds(0, rows)].reshape(size, DH) for block in blocks]
    grad = [qg_ref[block, pl.ds(rows, rows)].reshape(size, DH) for block in blocks]
    stamp = [(offsets + part * SHARD_MS).astype(jnp.float32) for part in range(RANGES)]
    top, inverse, row_dot = [None] * RANGES, [None] * RANGES, [None] * RANGES

    def add(ref, at, fresh, value):
        ref[at] = value if fresh else ref[at] + value

    def unrolled(body, carry):
        for step in range(span):
            carry = body(step, carry)
        return carry

    def score_step(part, step, top):
        place = pl.ds(part * size + step * TILE, TILE)
        found = dot_nt(keys[place], query[part])
        near = jnp.abs(jnp.tile(stamps[place], (1, size // DH)) - stamp[part]) <= RADIUS_MS
        found = jnp.where(near, found * (SCALE * LOG2E), NEG_FILL)
        scores[part, step] = found
        return jnp.maximum(top, jnp.max(found.reshape(TILE // 8, 8, size), axis=0))

    def weight_step(part, step, total):
        place = pl.ds(part * size + step * TILE, TILE)
        raised = jnp.exp2(scores[part, step] - top[part])
        scores[part, step] = raised
        add(total_t, part, step == 0, dot(values[place], raised.astype(jnp.bfloat16), ((0,), (0,))))
        return total + jnp.sum(raised.reshape(TILE // 8, 8, size), axis=0)

    def grad_step(part, step):
        place = pl.ds(part * size + step * TILE, TILE)
        weights = scores[part, step] * inverse[part]
        slopes = (weights * (dot_nt(values[place], grad[part]) - row_dot[part])).astype(jnp.bfloat16)
        fresh = part == 0
        add(value_sums, place, fresh, dot_nn(weights.astype(jnp.bfloat16), grad[part]))
        add(key_sums, place, fresh, dot_nn(slopes, query[part]))
        add(query_t, part, step == 0, dot(keys[place], slopes, ((0,), (0,))))

    def finish(part, total):
        inverse[part] = 1.0 / jnp.sum(total, axis=0, keepdims=True)
        attended_t = total_t[part] * inverse[part]
        row_dot[part] = jnp.sum(
            attended_t * grad[part].astype(jnp.float32).T, axis=0, keepdims=True
        )
        shape = (per, rows, DH)
        result_ref[blocks[part], pl.ds(0, rows)] = attended_t.T.astype(jnp.bfloat16).reshape(shape)

    def finish_query(part):
        low = (query_t[part] * SCALE).T.astype(jnp.bfloat16)
        result_ref[blocks[part], pl.ds(rows, rows)] = low.reshape(per, rows, DH)

    lowest = jnp.full((8, size), NEG_FILL, jnp.float32)
    zero = jnp.zeros((8, size), jnp.float32)
    found = unrolled(lambda step, c: score_step(0, step, c), lowest)
    top[0] = jnp.max(found, axis=0, keepdims=True)

    def second(step, carry):
        return weight_step(0, step, carry[0]), score_step(1, step, carry[1])

    total, found = unrolled(second, (zero, lowest))
    top[1] = jnp.max(found, axis=0, keepdims=True)
    finish(0, total)

    def third(step, carry):
        grad_step(0, step)
        return weight_step(1, step, carry)

    total = unrolled(third, zero)
    finish_query(0)
    finish(1, total)

    def fourth(step, carry):
        grad_step(1, step)
        return carry

    unrolled(fourth, 0)
    finish_query(1)
    for side, ref in enumerate((to_left_ref, own_sum_ref, to_right_ref)):
        for part in range(RANGES):
            place = pl.ds((side * RANGES + part) * size, size)
            shape = (per, rows, DH)
            ref[blocks[part], pl.ds(0, rows)] = (key_sums[place] * SCALE).astype(ref.dtype).reshape(shape)
            ref[blocks[part], pl.ds(rows, rows)] = value_sums[place].astype(ref.dtype).reshape(shape)


def attend(heads, stamped, query_grad, sides, result, sums, sizes):
    peers = stamped[0].shape[0]
    per = peers // RANGES
    rows = (stamped[0].shape[1] - STAMP_ROWS) // (2 * len(CHUNKS[0]))
    size = per * rows
    span = 2 * REACH + 1
    places = 3 * RANGES

    def piece(first):
        start = heads[0] - first
        return pl.BlockSpec((peers, 2 * rows, DH), lambda head: (0, start + head, 0))

    stamp_block = 2 * len(CHUNKS[0]) * rows // STAMP_ROWS
    stamp_spec = pl.BlockSpec((peers, STAMP_ROWS, DH), lambda head: (0, stamp_block, 0))
    old = [result[0], *sums[0]]
    firsts = [result[1]] + [sums[1]] * 3
    kinds = [jnp.bfloat16] * 4
    counts = [sizes[0]] + [sizes[1]] * 3
    fresh = [value is None for value in old]
    operands = [*stamped, query_grad[0], *sides[0]]
    in_specs = [stamp_spec] * 3 + [piece(first) for first in (query_grad[1], *sides[1])]
    aliases = {}
    for number, value in enumerate(old):
        if value is not None:
            aliases[len(operands)] = number
            operands.append(value)
            in_specs.append(pl.BlockSpec(memory_space=pl.ANY))

    return pl.pallas_call(
        functools.partial(attend_kernel, per, size, fresh),
        grid=(len(heads),),
        in_specs=in_specs,
        out_specs=[piece(first) for first in firsts],
        out_shape=[
            jax.ShapeDtypeStruct((peers, 2 * rows * count, DH), kind)
            for count, kind in zip(counts, kinds)
        ],
        input_output_aliases=aliases,
        scratch_shapes=[
            pltpu.VMEM((places * size, DH), jnp.float32),
            pltpu.VMEM((places * size, DH), jnp.bfloat16),
            pltpu.VMEM((places * size, DH), jnp.bfloat16),
            pltpu.VMEM((RANGES, span * size // TILE, TILE, size), jnp.float32),
            pltpu.VMEM((places * size, DH), jnp.float32),
            pltpu.VMEM((places * size, DH), jnp.float32),
            pltpu.VMEM((RANGES, DH, size), jnp.float32),
            pltpu.VMEM((RANGES, DH, size), jnp.float32),
        ],
        compiler_params=pltpu.CompilerParams(vmem_limit_bytes=VMEM_BYTES),
        cost_estimate=pl.CostEstimate(
            flops=1, bytes_accessed=1, transcendentals=0
        ),
        name="attend",
    )(*operands)


def swap(value):
    return lax.all_to_all(value, GROUP, split_axis=0, concat_axis=0, tiled=True)


def shifted(value, steps):
    count = lax.axis_size("col")
    first, last = max(0, -steps), min(count, count - steps)
    return lax.ppermute(value, "col", [(at, at + steps) for at in range(first, last)])


def after(value, *others):
    return lax.optimization_barrier((value, others))[0]


def on_device(video_query, audio_key, audio_value, grad_out, audio_time):
    peers = lax.axis_size(GROUP)
    rows, width = video_query.shape
    heads = width // DH // peers
    early, late = CHUNKS
    block = 2 * rows
    arrays = (audio_key, audio_value, video_query, grad_out)
    key_plan = [(which, head) for head in early for which in (0, 1)]
    mixed_plan = [(which, head) for head in early for which in (2, 3)]
    mixed_plan += [(which, head) for head in late for which in (0, 1)]
    query_plan = [(which, head) for head in late for which in (2, 3)]
    (key_pack,) = pack(arrays[:2], [key_plan], peers, audio_time)
    own = swap(key_pack)
    mixed_pack, query_pack = pack(arrays, [mixed_plan, query_plan], peers)
    mixed = swap(after(mixed_pack, own))
    left, right = shifted(own, 1), shifted(own, -1)
    sent = after(mixed[:, block * len(early) :], left, right)
    late_left, late_right = shifted(sent, 1), shifted(sent, -1)
    queries = swap(after(query_pack, mixed))

    def gather(sums, came):
        return sum(value.astype(jnp.float32) for value in (sums[1], *came)).astype(jnp.bfloat16)

    stamped = (left, own, right)
    result, *sums = attend(
        early, stamped, (mixed, 0), (stamped, (0, 0, 0)), (None, 0), ([None] * 3, 0),
        (heads + len(early), len(early)),
    )
    came = shifted(sums[0], -1), shifted(sums[2], 1)
    first = late[0]
    result, *late_sums = attend(
        late, stamped, (queries, first), ((late_left, mixed, late_right), (first, 0, first)),
        (result, 0), ([None] * 3, first), (heads + len(early), len(late)),
    )
    to_left, to_right = after((late_sums[0], late_sums[2]), came)
    late_came = shifted(to_left, -1), shifted(to_right, 1)
    result = lax.dynamic_update_slice(result, gather(sums, came), (0, block * heads, 0))
    result = swap(result)
    grads = swap(gather(late_sums, late_came))
    attended = place(result, 0, early + late, heads, rows)
    grad = place(result, block * heads, early, heads, rows)
    return (*attended, *place(grads, 0, late, heads, rows, grad))


def solution(mesh):
    columns = mesh.shape["seq"] // RANGES
    split = Mesh(
        mesh.devices.reshape(columns, RANGES, mesh.shape["head"]), ("col", "yh", "head")
    )
    rows = P(("col", "yh", "head"), None)
    return jax.shard_map(
        on_device,
        mesh=split,
        in_specs=(rows, rows, rows, rows, P(("col", "yh", "head"))),
        out_specs=(rows, rows, rows, rows),
        check_vma=False,
    )
```
